1024 devices in a mesh: dp: 64 (over x, z_lo), mp: 16 (over z_hi, y, core).
Axes of the slice: x: 4, y: 4, z: 32 (z_hi: 2, z_lo: 16; z = z_hi * 16 + z_lo), core: 2. Of those that a mesh axis runs over, the one named last changes fastest.
Arguments:
- cotangent: bfloat16 [49152, 4096], P('dp'), may hold values from -6 to 6
- activations: bfloat16 [49152, 16384], P('dp', 'mp'), may hold values from -32 to 32
- live_mask: int32 [49152], P('dp'), may hold values 0 or 1
- projector: bfloat16 [4096, 256], replicated, may hold values from -0.09375 to 0.09375
- first_moment: float32 [16384, 256], P(('mp', 'dp')), may hold values from -4 to 4
- second_moment: float32 [16384, 256], P(('mp', 'dp')), may hold values from 0.05 to 2
Outputs:
- new_first: float32 [16384, 256], P(('mp', 'dp'))
- new_second: float32 [16384, 256], P(('mp', 'dp'))
- update: bfloat16 [4096, 16384], P('dp', 'mp')
The draws below stay inside these ranges and needn't reach their ends.
All inputs are finite; a program needn't handle non-finite values. No bound on the sum of `live_mask` on one device may be relied on, other than what follows from the above.
Results may differ from the reference program's by a relative error of at most 0.0053.
Values may be sent and summed in bfloat16 or wider, within the bound.
No kernel may reach another device: no remote copies, remote signals or barrier semaphores. Data moves between devices by JAX's collectives and lax.ppermute only.
A program may use at most 32 MiB of HBM per device.

```python
import math
import jax
import jax.numpy as jnp
from jax import lax

D = 4096
FF = 16384
RANK = 256
TOKENS = 49152


def plant(array, rng, low, high):
    place = [jax.random.randint(jax.random.fold_in(rng, axis), (), 0, length) for axis, length in enumerate(array.shape)]
    main_axis = array.shape.index(max(array.shape))
    next_to = place[:main_axis] + [(place[main_axis] + 1) % array.shape[main_axis]] + place[main_axis + 1:]
    return array.at[tuple(place)].set(low).at[tuple(next_to)].set(high)


def spiked(array, key, source, target, shards_of, factor):
    def block_of(dim):
        return (jnp.arange(array.shape[dim]) // (array.shape[dim] // shards_of)).reshape((-1,) + (1,) * (array.ndim - 1 - dim))

    first = jax.random.permutation(key, shards_of)[block_of(target)]
    far = (block_of(target) + shards_of // 2) % shards_of
    return jnp.where((block_of(source) == first) | (block_of(source) == far), factor * array, array)


def block_scale(own_key, shape, cuts, least, top_value):
    loudness = 1.0
    for axis_at, shards_of in cuts:
        draws = jax.random.uniform(jax.random.fold_in(jax.random.fold_in(own_key, 6), axis_at), (shards_of,), jnp.float32, least / len(cuts), top_value / len(cuts))
        loudness = loudness * jnp.repeat(jnp.exp(draws), shape[axis_at] // shards_of).reshape((-1,) + (1,) * (len(shape) - 1 - axis_at))
    return loudness


def centred(own_key, extent, scale, bound, pieces=(), held_as=jnp.bfloat16):
    factor_of = block_scale(own_key, extent, pieces, -0.22, 0.18) if pieces else 1.0
    result = jax.random.normal(own_key, extent, jnp.float32) * scale * factor_of
    return jnp.minimum(jnp.maximum(result, -bound), bound).astype(held_as)


def heavy_noise(own_key, dims, deviation, most, cuts, heavy, held_as=jnp.bfloat16):
    array = deviation * jax.random.normal(own_key, dims, jnp.float32)
    if cuts:
        array = array * block_scale(own_key, dims, cuts, -0.22, 0.18)
    return jnp.clip(spiked(array, jax.random.fold_in(own_key, 3), *heavy), -most, most).astype(held_as)


def setup_inputs(seed: int = 0) -> dict:
    streams_of = jax.random.split(jax.random.key(seed), 7)
    cotangent = centred(streams_of[0], (TOKENS, D), 1.0, 6.0, ((0, 64),))
    activations = heavy_noise(streams_of[1], (TOKENS, FF), 2.0, 32.0, ((0, 64), (1, 16)), (0, 1, 64, 4.0))
    live_mask = plant((jax.random.randint(streams_of[2], (TOKENS,), 0, 4) < 3).astype(jnp.int32), jax.random.fold_in(streams_of[2], 1), 0, 1)
    projector = centred(streams_of[3], (D, RANK), D ** -0.5, 0.09375)
    first_moment = centred(streams_of[4], (FF, RANK), 0.5, 4.0, ((0, 1024),), jnp.float32)
    second_moment = jnp.clip(jnp.exp(math.log(2.0) - 3.6888794 * jax.random.uniform(streams_of[5], (FF, RANK), jnp.float32) ** block_scale(streams_of[5], (FF, RANK), ((0, 1024),), -0.2, 0.2)), 0.05, 2.0)
    return dict(cotangent=cotangent, activations=activations, live_mask=live_mask, projector=projector, first_moment=first_moment, second_moment=second_moment)


beta_one = 0.9
beta_two = 0.95
corr_one = 0.99997343860111
corr_two = 0.99407947077967
adam_eps = 1e-08

def reference(cotangent, activations, live_mask, projector, first_moment, second_moment):
    projected = jnp.dot(cotangent, projector, preferred_element_type=jnp.float32)
    weighted = (projected * live_mask.astype(jnp.float32)[:, None]).astype(jnp.bfloat16)
    gradient = lax.dot_general(activations, weighted, (((0,), (0,)), ((), ())), preferred_element_type=jnp.float32)
    gradient = gradient * jnp.float32(1.0 / TOKENS ** 0.5)
    new_first = beta_one * first_moment + (1.0 - beta_one) * gradient
    new_second = beta_two * second_moment + (1.0 - beta_two) * gradient * gradient
    direction = (new_first / corr_one / (jnp.sqrt(new_second / corr_two) + adam_eps)).astype(jnp.bfloat16)
    update = lax.dot_general(projector, direction, (((1,), (1,)), ((), ())), preferred_element_type=jnp.float32)
    return (new_first, new_second, update.astype(jnp.bfloat16))
```

```python
import math

import jax
import jax.numpy as jnp
from jax import lax
from jax.experimental import pallas as pl
from jax.experimental.pallas import tpu as pltpu
from jax.sharding import PartitionSpec as P

beta_one = 0.9
beta_two = 0.95
corr_one = 0.99997343860111
corr_two = 0.99407947077967
adam_eps = 1e-08

NEAR = [[16 * x + 4 * a + b for x in range(4) for b in range(4)] for a in range(4)]
SWAP_EIGHT = [(d, d ^ 8) for d in range(64)]
SWAP_FOUR = [(d, d ^ 4) for d in range(64)]


def adam(first, second, gradient):
    new_first = beta_one * first + (1.0 - beta_one) * gradient
    new_second = beta_two * second + (1.0 - beta_two) * gradient * gradient
    direction = new_first / corr_one / (jnp.sqrt(new_second / corr_two) + adam_eps)
    return new_first, new_second, direction.astype(jnp.bfloat16)


def order_kernel(blocks_ref, update_ref):
    _, _, length = blocks_ref.shape
    rows = length // 4
    source = lax.broadcasted_iota(jnp.int32, (length, 4 * length), 0)
    target = lax.broadcasted_iota(jnp.int32, (length, 4 * length), 1)
    start = (source // rows) * length + source % rows
    for x in range(4):
        total = None
        for b in range(4):
            place = (target == start + b * rows).astype(jnp.bfloat16)
            moved = jnp.dot(blocks_ref[4 * x + b], place, preferred_element_type=jnp.float32)
            total = moved if total is None else total + moved
        update_ref[:, x * 4 * length : (x + 1) * 4 * length] = total.astype(jnp.bfloat16)


def per_device(cotangent, activations, live_mask, projector, first_moment, second_moment):
    width, rank = projector.shape
    own = lax.axis_index("dp")
    projected = jnp.dot(cotangent, projector, preferred_element_type=jnp.float32)
    weighted = (projected * live_mask.astype(jnp.float32)[:, None]).astype(jnp.bfloat16)
    factor = 1.0 / math.sqrt(activations.shape[0] * lax.axis_size("dp"))
    term = lax.dot_general(
        activations, weighted, (((0,), (0,)), ((), ())), preferred_element_type=jnp.float32
    )
    rows = term.shape[0] // 64
    term = (term * jnp.float32(factor)).astype(jnp.bfloat16)
    parts = term.reshape(4, 4, 4, rows, rank).transpose(0, 2, 1, 3, 4).reshape(16, 4 * rows, rank)
    parts = lax.all_to_all(parts, "dp", 0, 0, axis_index_groups=NEAR, tiled=True)
    partial = jnp.sum(parts.astype(jnp.float32), axis=0)

    def swap(pairs, sums, first, second, low):
        note = jnp.concatenate([sums, first, second], axis=0).astype(jnp.bfloat16)
        other = lax.ppermute(note, "dp", pairs).astype(jnp.float32)
        ends = (sums.shape[0], sums.shape[0] + first.shape[0])
        firsts, seconds = other[ends[0] : ends[1]], other[ends[1] :]

        def pair(mine, yours):
            mine, yours = mine.reshape(-1, rows, rank), yours.reshape(-1, rows, rank)
            both = jnp.stack([jnp.where(low, mine, yours), jnp.where(low, yours, mine)], axis=1)
            return both.reshape(-1, rank)

        return sums + other[: ends[0]], pair(first, firsts), pair(second, seconds)

    low_eight, low_four = (own // 8) % 2 == 0, (own // 4) % 2 == 0
    gradient, firsts, seconds = swap(SWAP_EIGHT, partial, first_moment, second_moment, low_eight)
    gradient, firsts, seconds = swap(SWAP_FOUR, gradient, firsts, seconds, low_four)
    all_first, all_second, direction = adam(firsts, seconds, gradient)
    own_far = (own // 4) % 4
    new_first = lax.dynamic_slice_in_dim(all_first, own_far * rows, rows, 0)
    new_second = lax.dynamic_slice_in_dim(all_second, own_far * rows, rows, 0)
    band = width // 64
    bands = lax.dynamic_index_in_dim(projector.reshape(4, 4, 4, band, rank), own_far, 1, False)
    blocks = lax.dot_general(
        bands.reshape(16 * band, rank), direction, (((1,), (1,)), ((), ())), preferred_element_type=jnp.float32
    ).astype(jnp.bfloat16).reshape(16, band, 4 * rows)
    blocks = lax.all_to_all(blocks, "dp", 0, 0, axis_index_groups=NEAR, tiled=True)
    update = pl.pallas_call(
        order_kernel,
        out_shape=jax.ShapeDtypeStruct((band, 64 * rows), jnp.bfloat16),
        in_specs=[pl.BlockSpec(memory_space=pltpu.VMEM)],
        out_specs=pl.BlockSpec(memory_space=pltpu.VMEM),
    )(blocks)
    return (new_first, new_second, update)


def solution(mesh):
    in_specs = (
        P("dp", None),
        P("dp", "mp"),
        P("dp"),
        P(),
        P(("mp", "dp"), None),
        P(("mp", "dp"), None),
    )
    out_specs = (P(("mp", "dp"), None), P(("mp", "dp"), None), P("dp", "mp"))
    return jax.shard_map(
        per_device, mesh=mesh, in_specs=in_specs, out_specs=out_specs, check_vma=False
    )
```

```python
import functools
import math

import jax
import jax.numpy as jnp
from jax import lax
from jax.experimental import pallas as pl
from jax.experimental.pallas import tpu as pltpu
from jax.sharding import PartitionSpec as P

beta_one = 0.9
beta_two = 0.95
corr_one = 0.99997343860111
corr_two = 0.99407947077967
adam_eps = 1e-08

NEAR = [[16 * x + 4 * a + b for x in range(4) for b in range(4)] for a in range(4)]
FAR = [[16 * x + 4 * a + b for a in range(4)] for x in range(4) for b in range(4)]
SWAP_EIGHT = [(d, d ^ 8) for d in range(64)]
SWAP_FOUR = [(d, d ^ 4) for d in range(64)]


WIDTH_STEP = 1024


def adam(first, second, gradient):
    new_first = beta_one * first + (1.0 - beta_one) * gradient
    new_second = beta_two * second + (1.0 - beta_two) * gradient * gradient
    direction = new_first / corr_one / (jnp.sqrt(new_second / corr_two) + adam_eps)
    return new_first, new_second, direction.astype(jnp.bfloat16)


def term_kernel(factor, mask_ref, cot_hbm, act_hbm, proj_hbm, parts_ref, cot, act, turned, proj, total, cot_sem, act_sem, proj_sem):
    tokens, width = cot.shape
    hidden, rank = act.shape[1], proj.shape[1]
    pieces = width // WIDTH_STEP

    def cot_copy(k):
        at = (slice(None), pl.ds(k * WIDTH_STEP, WIDTH_STEP))
        return pltpu.make_async_copy(cot_hbm.at[at], cot.at[at], cot_sem.at[k])

    def proj_copy(k):
        at = pl.ds(k * WIDTH_STEP, WIDTH_STEP)
        return pltpu.make_async_copy(proj_hbm.at[at], proj.at[at], proj_sem.at[k])

    act_copy = pltpu.make_async_copy(act_hbm, act, act_sem)
    ahead = 2

    def start(k):
        if k < pieces:
            proj_copy(k).start()
            cot_copy(k).start()
        if k == 0:
            act_copy.start()

    for k in range(ahead):
        start(k)
    ones = jnp.ones((8, rank), jnp.bfloat16)
    mask = jnp.broadcast_to(mask_ref[...].astype(jnp.float32)[None, :], (8, tokens))
    mask8 = jnp.where(lax.broadcasted_iota(jnp.int32, mask.shape, 0) == 0, mask, 0.0)
    live = lax.dot_general(
        mask8.astype(jnp.bfloat16), ones, (((0,), (0,)), ((), ())), preferred_element_type=jnp.float32
    )
    for k in range(pieces):
        proj_copy(k).wait()
        cot_copy(k).wait()
        start(k + ahead)
        columns = slice(k * WIDTH_STEP, (k + 1) * WIDTH_STEP)
        piece = jnp.dot(cot[:, columns], proj[columns, :], preferred_element_type=jnp.float32)
        if k > 0:
            piece = total[...] + piece
        if k < pieces - 1:
            total[...] = piece
        if k == 0:
            act_copy.wait()
        if k >= 0:
            each = hidden // (pieces - 0)
            units = slice((k - 0) * each, (k - 0 + 1) * each)
            turned[units, :] = act[:, units].T
    weighted = (piece * live).astype(jnp.bfloat16)
    for x in range(4):
        units = slice(x * hidden // 4, (x + 1) * hidden // 4)
        piece = jnp.dot(turned[units, :], weighted, preferred_element_type=jnp.float32)
        done = (piece * factor).astype(jnp.bfloat16).reshape(4, 4, hidden // 64, rank)
        for b in range(4):
            parts_ref[4 * x + b] = done[:, b].reshape(hidden // 16, rank)


def order_kernel(blocks_ref, update_ref):
    _, half, length = blocks_ref.shape
    units = length // 2
    rows = units // 4
    source = lax.broadcasted_iota(jnp.int32, (length, 4 * units), 0)
    target = lax.broadcasted_iota(jnp.int32, (length, 4 * units), 1)
    for side in range(2):
        inside = source - side * units
        start = (inside // rows) * units + inside % rows
        valid = (inside >= 0) & (inside < units)
        total = None
        for b in range(4):
            place = (valid & (target == start + b * rows)).astype(jnp.float32).astype(jnp.bfloat16)
            stacked = jnp.concatenate([blocks_ref[4 * x + b] for x in range(4)], axis=0)
            moved = jnp.dot(stacked, place, preferred_element_type=jnp.float32)
            total = moved if total is None else total + moved
        total = total.astype(jnp.bfloat16)
        for x in range(4):
            update_ref[side * half : (side + 1) * half, x * 4 * units : (x + 1) * 4 * units] = total[
                x * half : (x + 1) * half, :
            ]


def per_device(cotangent, activations, live_mask, projector, first_moment, second_moment):
    width, rank = projector.shape
    own = lax.axis_index("dp")
    tokens, hidden = activations.shape
    rows, pieces = hidden // 64, width // WIDTH_STEP
    factor = 1.0 / math.sqrt(tokens * lax.axis_size("dp"))
    vmem, hbm = pl.BlockSpec(memory_space=pltpu.VMEM), pl.BlockSpec(memory_space=pltpu.HBM)
    parts = pl.pallas_call(
        functools.partial(term_kernel, factor),
        out_shape=jax.ShapeDtypeStruct((16, 4 * rows, rank), jnp.bfloat16),
        in_specs=[vmem, hbm, hbm, hbm],
        out_specs=vmem,
        scratch_shapes=[
            pltpu.VMEM((tokens, width), jnp.bfloat16),
            pltpu.VMEM((tokens, hidden), jnp.bfloat16),
            pltpu.VMEM((hidden, tokens), jnp.bfloat16),
            pltpu.VMEM((width, rank), jnp.bfloat16),
            pltpu.VMEM((tokens, rank), jnp.float32),
            pltpu.SemaphoreType.DMA((pieces,)),
            pltpu.SemaphoreType.DMA,
            pltpu.SemaphoreType.DMA((pieces,)),
        ],
        compiler_params=pltpu.CompilerParams(vmem_limit_bytes=60 * 2**20),
        name="term",
    )(live_mask, cotangent, activations, projector)
    parts = lax.all_to_all(parts, "dp", 0, 0, axis_index_groups=NEAR, tiled=True)
    partial = jnp.sum(parts.astype(jnp.float32), axis=0)

    def swap(pairs, sums, first, second, low):
        note = jnp.concatenate([sums, first, second], axis=0).astype(jnp.bfloat16)
        other = lax.ppermute(note, "dp", pairs).astype(jnp.float32)
        ends = (sums.shape[0], sums.shape[0] + first.shape[0])
        firsts, seconds = other[ends[0] : ends[1]], other[ends[1] :]

        def pair(mine, yours):
            mine, yours = mine.reshape(-1, rows, rank), yours.reshape(-1, rows, rank)
            both = jnp.stack([jnp.where(low, mine, yours), jnp.where(low, yours, mine)], axis=1)
            return both.reshape(-1, rank)

        return sums + other[: ends[0]], pair(first, firsts), pair(second, seconds)

    low_eight, low_four = (own // 8) % 2 == 0, (own // 4) % 2 == 0
    gradient, firsts, seconds = swap(SWAP_EIGHT, partial, first_moment, second_moment, low_eight)
    gradient, firsts, seconds = swap(SWAP_FOUR, gradient, firsts, seconds, low_four)
    all_first, all_second, direction = adam(firsts, seconds, gradient)
    own_far = (own // 4) % 4
    new_first = lax.dynamic_slice_in_dim(all_first, own_far * rows, rows, 0)
    new_second = lax.dynamic_slice_in_dim(all_second, own_far * rows, rows, 0)
    band = width // 64
    bands = lax.dynamic_index_in_dim(projector.reshape(4, 4, 4, band, rank), own_far, 1, False)
    blocks = lax.dot_general(
        bands.reshape(16 * band, rank), direction, (((1,), (1,)), ((), ())), preferred_element_type=jnp.float32
    ).astype(jnp.bfloat16).reshape(16, 2, band // 2, 4 * rows)
    blocks = jnp.concatenate([blocks[:, 0], blocks[:, 1]], axis=-1)
    blocks = lax.all_to_all(blocks, "dp", 0, 0, axis_index_groups=NEAR, tiled=True)
    update = pl.pallas_call(
        order_kernel,
        out_shape=jax.ShapeDtypeStruct((band, 64 * rows), jnp.bfloat16),
        in_specs=[vmem],
        out_specs=vmem,
        compiler_params=pltpu.CompilerParams(vmem_limit_bytes=4 * 2**20),
        name="order",
    )(blocks)
    return (new_first, new_second, update)


def solution(mesh):
    in_specs = (
        P("dp", None),
        P("dp", "mp"),
        P("dp"),
        P(),
        P(("mp", "dp"), None),
        P(("mp", "dp"), None),
    )
    out_specs = (P(("mp", "dp"), None), P(("mp", "dp"), None), P("dp", "mp"))
    return jax.shard_map(
        per_device, mesh=mesh, in_specs=in_specs, out_specs=out_specs, check_vma=False
    )
```

```python
import functools
import math

import jax
import jax.numpy as jnp
from jax import lax
from jax.experimental import pallas as pl
from jax.experimental.pallas import tpu as pltpu
from jax.sharding import PartitionSpec as P

beta_one = 0.9
beta_two = 0.95
corr_one = 0.99997343860111
corr_two = 0.99407947077967
adam_eps = 1e-08

NEAR = [[16 * x + 4 * a + b for x in range(4) for b in range(4)] for a in range(4)]
FAR = [[16 * x + 4 * a + b for a in range(4)] for x in range(4) for b in range(4)]
SWAP_EIGHT = [(d, d ^ 8) for d in range(64)]
SWAP_FOUR = [(d, d ^ 4) for d in range(64)]


WIDTH_STEP = 1024


def adam(first, second, gradient):
    new_first = beta_one * first + (1.0 - beta_one) * gradient
    new_second = beta_two * second + (1.0 - beta_two) * gradient * gradient
    direction = new_first / corr_one / (jnp.sqrt(new_second / corr_two) + adam_eps)
    return new_first, new_second, direction.astype(jnp.bfloat16)


def term_kernel(factor, mask_ref, cot_hbm, act_hbm, proj_hbm, parts_ref, cot, act, turned, proj, total, cot_sem, act_sem, proj_sem):
    tokens, width = cot.shape
    hidden, rank = act.shape[1], proj.shape[1]
    pieces = width // WIDTH_STEP

    def cot_copy(k):
        at = (slice(None), pl.ds(k * WIDTH_STEP, WIDTH_STEP))
        return pltpu.make_async_copy(cot_hbm.at[at], cot.at[at], cot_sem.at[k])

    def proj_copy(k):
        at = pl.ds(k * WIDTH_STEP, WIDTH_STEP)
        return pltpu.make_async_copy(proj_hbm.at[at], proj.at[at], proj_sem.at[k])

    act_copy = pltpu.make_async_copy(act_hbm, act, act_sem)
    ahead = 2

    def start(k):
        if k < pieces:
            proj_copy(k).start()
            cot_copy(k).start()
        if k == 0:
            act_copy.start()

    for k in range(ahead):
        start(k)
    ones = jnp.ones((8, rank), jnp.bfloat16)
    mask = jnp.broadcast_to(mask_ref[...].astype(jnp.float32)[None, :], (8, tokens))
    mask8 = jnp.where(lax.broadcasted_iota(jnp.int32, mask.shape, 0) == 0, mask, 0.0)
    live = lax.dot_general(
        mask8.astype(jnp.bfloat16), ones, (((0,), (0,)), ((), ())), preferred_element_type=jnp.float32
    )
    for k in range(pieces):
        proj_copy(k).wait()
        cot_copy(k).wait()
        start(k + ahead)
        columns = slice(k * WIDTH_STEP, (k + 1) * WIDTH_STEP)
        piece = jnp.dot(cot[:, columns], proj[columns, :], preferred_element_type=jnp.float32)
        if k > 0:
            piece = total[...] + piece
        if k < pieces - 1:
            total[...] = piece
        if k == 0:
            act_copy.wait()
        if k >= 0:
            each = hidden // (pieces - 0)
            units = slice((k - 0) * each, (k - 0 + 1) * each)
            turned[units, :] = act[:, units].T
    weighted = (piece * live).astype(jnp.bfloat16)
    for x in range(4):
        units = slice(x * hidden // 4, (x + 1) * hidden // 4)
        piece = jnp.dot(turned[units, :], weighted, preferred_element_type=jnp.float32)
        done = (piece * factor).astype(jnp.bfloat16).reshape(4, 4, hidden // 64, rank)
        for b in range(4):
            parts_ref[4 * x + b] = done[:, b].reshape(hidden // 16, rank)


def step_kernel(sums_ref, first_ref, second_ref, other_ref, bands_ref, new_first_ref, new_second_ref, blocks_ref):
    own_far = (lax.axis_index("dp") // 4) % 4
    mine = own_far % 2
    units, rank = sums_ref.shape
    rows = units // 4
    directions = []
    for a in range(4):
        here = mine == a % 2
        at = slice((a // 2) * rows, (a // 2 + 1) * rows)
        gradient = sums_ref[a * rows : (a + 1) * rows, :] + other_ref[a * rows : (a + 1) * rows, :].astype(jnp.float32)
        start = units + (a // 2) * rows
        yours = other_ref[start : start + rows, :].astype(jnp.float32)
        first = jnp.where(here, first_ref[at, :], yours)
        yours = other_ref[start + 2 * rows : start + 3 * rows, :].astype(jnp.float32)
        second = jnp.where(here, second_ref[at, :], yours)
        new_first, new_second, direction = adam(first, second, gradient)
        directions.append(direction)
        if a == 0:
            own_first, own_second = new_first, new_second
        else:
            own_first = jnp.where(own_far == a, new_first, own_first)
            own_second = jnp.where(own_far == a, new_second, own_second)
    new_first_ref[...] = own_first
    new_second_ref[...] = own_second
    direction = jnp.concatenate(directions, axis=0)
    none = jnp.zeros_like(direction)
    low, high = jnp.concatenate([direction, none], axis=0), jnp.concatenate([none, direction], axis=0)
    peers, band, _ = bands_ref.shape
    half = band // 2
    down = (((1,), (1,)), ((), ()))
    top = bands_ref[:, :half, :].reshape(peers * half, rank)
    bottom = bands_ref[:, half:, :].reshape(peers * half, rank)
    both = lax.dot_general(top, low, down, preferred_element_type=jnp.float32)
    both += lax.dot_general(bottom, high, down, preferred_element_type=jnp.float32)
    blocks_ref[...] = both.astype(jnp.bfloat16).reshape(peers, half, 2 * units)


def order_kernel(blocks_ref, update_ref):
    _, half, length = blocks_ref.shape
    units = length // 2
    rows = units // 4
    source = lax.broadcasted_iota(jnp.int32, (length, 4 * units), 0)
    target = lax.broadcasted_iota(jnp.int32, (length, 4 * units), 1)
    for side in range(2):
        inside = source - side * units
        start = (inside // rows) * units + inside % rows
        valid = (inside >= 0) & (inside < units)
        total = None
        for b in range(4):
            place = (valid & (target == start + b * rows)).astype(jnp.float32).astype(jnp.bfloat16)
            stacked = jnp.concatenate([blocks_ref[4 * x + b] for x in range(4)], axis=0)
            moved = jnp.dot(stacked, place, preferred_element_type=jnp.float32)
            total = moved if total is None else total + moved
        total = total.astype(jnp.bfloat16)
        for x in range(4):
            update_ref[side * half : (side + 1) * half, x * 4 * units : (x + 1) * 4 * units] = total[
                x * half : (x + 1) * half, :
            ]


def per_device(cotangent, activations, live_mask, projector, first_moment, second_moment):
    width, rank = projector.shape
    own = lax.axis_index("dp")
    tokens, hidden = activations.shape
    rows, pieces = hidden // 64, width // WIDTH_STEP
    factor = 1.0 / math.sqrt(tokens * lax.axis_size("dp"))
    vmem, hbm = pl.BlockSpec(memory_space=pltpu.VMEM), pl.BlockSpec(memory_space=pltpu.HBM)
    parts = pl.pallas_call(
        functools.partial(term_kernel, factor),
        out_shape=jax.ShapeDtypeStruct((16, 4 * rows, rank), jnp.bfloat16),
        in_specs=[vmem, hbm, hbm, hbm],
        out_specs=vmem,
        scratch_shapes=[
            pltpu.VMEM((tokens, width), jnp.bfloat16),
            pltpu.VMEM((tokens, hidden), jnp.bfloat16),
            pltpu.VMEM((hidden, tokens), jnp.bfloat16),
            pltpu.VMEM((width, rank), jnp.bfloat16),
            pltpu.VMEM((tokens, rank), jnp.float32),
            pltpu.SemaphoreType.DMA((pieces,)),
            pltpu.SemaphoreType.DMA,
            pltpu.SemaphoreType.DMA((pieces,)),
        ],
        compiler_params=pltpu.CompilerParams(vmem_limit_bytes=60 * 2**20),
        name="term",
    )(live_mask, cotangent, activations, projector)
    parts = lax.all_to_all(parts, "dp", 0, 0, axis_index_groups=NEAR, tiled=True)
    partial = jnp.sum(parts.astype(jnp.float32), axis=0)

    def swap(pairs, sums, first, second):
        note = jnp.concatenate([sums, first, second], axis=0).astype(jnp.bfloat16)
        return lax.ppermute(note, "dp", pairs)

    other = swap(SWAP_EIGHT, partial, first_moment, second_moment).astype(jnp.float32)
    sums = partial + other[: 4 * rows]
    own_far = (own // 4) % 4
    low = own_far < 2

    def pair(mine, yours):
        return jnp.concatenate([jnp.where(low, mine, yours), jnp.where(low, yours, mine)], axis=0)

    first = pair(first_moment, other[4 * rows : 5 * rows])
    second = pair(second_moment, other[5 * rows :])
    other = swap(SWAP_FOUR, sums, first, second)
    band = width // 64
    bands = lax.dynamic_index_in_dim(projector.reshape(4, 4, 4, band, rank), own_far, 1, False)
    new_first, new_second, blocks = pl.pallas_call(
        step_kernel,
        out_shape=[
            jax.ShapeDtypeStruct((rows, rank), jnp.float32),
            jax.ShapeDtypeStruct((rows, rank), jnp.float32),
            jax.ShapeDtypeStruct((16, band // 2, 8 * rows), jnp.bfloat16),
        ],
        in_specs=[vmem] * 5,
        out_specs=[vmem] * 3,
        compiler_params=pltpu.CompilerParams(vmem_limit_bytes=8 * 2**20),
        name="step",
    )(sums, first, second, other, bands.reshape(16, band, rank))
    blocks = lax.all_to_all(blocks, "dp", 0, 0, axis_index_groups=NEAR, tiled=True)
    update = pl.pallas_call(
        order_kernel,
        out_shape=jax.ShapeDtypeStruct((band, 64 * rows), jnp.bfloat16),
        in_specs=[vmem],
        out_specs=vmem,
        compiler_params=pltpu.CompilerParams(vmem_limit_bytes=4 * 2**20),
        name="order",
    )(blocks)
    return (new_first, new_second, update)


def solution(mesh):
    in_specs = (
        P("dp", None),
        P("dp", "mp"),
        P("dp"),
        P(),
        P(("mp", "dp"), None),
        P(("mp", "dp"), None),
    )
    out_specs = (P(("mp", "dp"), None), P(("mp", "dp"), None), P("dp", "mp"))
    return jax.shard_map(
        per_device, mesh=mesh, in_specs=in_specs, out_specs=out_specs, check_vma=False
    )
```

```python
import functools
import math

import jax
import jax.numpy as jnp
from jax import lax
from jax.experimental import pallas as pl
from jax.experimental.pallas import tpu as pltpu
from jax.sharding import PartitionSpec as P

beta_one = 0.9
beta_two = 0.95
corr_one = 0.99997343860111
corr_two = 0.99407947077967
adam_eps = 1e-08

NEAR = [[16 * x + 4 * a + b for x in range(4) for b in range(4)] for a in range(4)]
FAR = [[16 * x + 4 * a + b for a in range(4)] for x in range(4) for b in range(4)]
SWAP_EIGHT = [(d, d ^ 8) for d in range(64)]
SWAP_FOUR = [(d, d ^ 4) for d in range(64)]


WIDTH_STEP = 1024


def adam(first, second, gradient):
    new_first = beta_one * first + (1.0 - beta_one) * gradient
    new_second = beta_two * second + (1.0 - beta_two) * gradient * gradient
    direction = new_first / corr_one / (jnp.sqrt(new_second / corr_two) + adam_eps)
    return new_first, new_second, direction.astype(jnp.bfloat16)


def term_kernel(factor, mask_ref, cot_hbm, act_hbm, proj_hbm, parts_ref, cot, act, turned, proj, total, cot_sem, act_sem, proj_sem):
    tokens, width = cot.shape
    hidden, rank = act.shape[1], proj.shape[1]
    pieces = width // WIDTH_STEP

    def cot_copy(k):
        at = (slice(None), pl.ds(k * WIDTH_STEP, WIDTH_STEP))
        return pltpu.make_async_copy(cot_hbm.at[at], cot.at[at], cot_sem.at[k])

    def proj_copy(k):
        at = pl.ds(k * WIDTH_STEP, WIDTH_STEP)
        return pltpu.make_async_copy(proj_hbm.at[at], proj.at[at], proj_sem.at[k])

    act_copy = pltpu.make_async_copy(act_hbm, act, act_sem)
    ahead = 3

    def start(k):
        if k < pieces:
            proj_copy(k).start()
            cot_copy(k).start()
        if k == 0:
            act_copy.start()

    for k in range(ahead):
        start(k)
    ones = jnp.ones((8, rank), jnp.bfloat16)
    mask = jnp.broadcast_to(mask_ref[...].astype(jnp.float32)[None, :], (8, tokens))
    mask8 = jnp.where(lax.broadcasted_iota(jnp.int32, mask.shape, 0) == 0, mask, 0.0)
    live = lax.dot_general(
        mask8.astype(jnp.bfloat16), ones, (((0,), (0,)), ((), ())), preferred_element_type=jnp.float32
    )
    for k in range(pieces):
        proj_copy(k).wait()
        cot_copy(k).wait()
        start(k + ahead)
        columns = slice(k * WIDTH_STEP, (k + 1) * WIDTH_STEP)
        piece = jnp.dot(cot[:, columns], proj[columns, :], preferred_element_type=jnp.float32)
        if k > 0:
            piece = total[...] + piece
        if k < pieces - 1:
            total[...] = piece
        if k == 0:
            act_copy.wait()
        if k >= 0:
            each = hidden // (pieces - 0)
            units = slice((k - 0) * each, (k - 0 + 1) * each)
            turned[units, :] = act[:, units].T
    weighted = (piece * live).astype(jnp.bfloat16)
    for x in range(4):
        units = slice(x * hidden // 4, (x + 1) * hidden // 4)
        piece = jnp.dot(turned[units, :], weighted, preferred_element_type=jnp.float32)
        done = (piece * factor).astype(jnp.bfloat16).reshape(4, 4, hidden // 64, rank)
        for b in range(4):
            parts_ref[4 * x + b] = done[:, b].reshape(hidden // 16, rank)


def step_kernel(sums_ref, first_ref, second_ref, other_ref, bands_ref, new_first_ref, new_second_ref, blocks_ref):
    own_far = (lax.axis_index("dp") // 4) % 4
    mine = own_far % 2
    units, rank = sums_ref.shape
    rows = units // 4
    directions = []
    for a in range(4):
        here = mine == a % 2
        at = slice((a // 2) * rows, (a // 2 + 1) * rows)
        gradient = sums_ref[a * rows : (a + 1) * rows, :] + other_ref[a * rows : (a + 1) * rows, :].astype(jnp.float32)
        start = units + (a // 2) * rows
        yours = other_ref[start : start + rows, :].astype(jnp.float32)
        first = jnp.where(here, first_ref[at, :], yours)
        yours = other_ref[start + 2 * rows : start + 3 * rows, :].astype(jnp.float32)
        second = jnp.where(here, second_ref[at, :], yours)
        new_first, new_second, direction = adam(first, second, gradient)
        directions.append(direction)
        if a == 0:
            own_first, own_second = new_first, new_second
        else:
            own_first = jnp.where(own_far == a, new_first, own_first)
            own_second = jnp.where(own_far == a, new_second, own_second)
    new_first_ref[...] = own_first
    new_second_ref[...] = own_second
    direction = jnp.concatenate(directions, axis=0)
    none = jnp.zeros_like(direction)
    low, high = jnp.concatenate([direction, none], axis=0), jnp.concatenate([none, direction], axis=0)
    peers, band, _ = bands_ref.shape
    half = band // 2
    down = (((1,), (1,)), ((), ()))
    top = bands_ref[:, :half, :].reshape(peers * half, rank)
    bottom = bands_ref[:, half:, :].reshape(peers * half, rank)
    both = lax.dot_general(top, low, down, preferred_element_type=jnp.float32)
    both += lax.dot_general(bottom, high, down, preferred_element_type=jnp.float32)
    blocks_ref[...] = both.astype(jnp.bfloat16).reshape(peers, half, 2 * units)


def order_kernel(blocks_ref, update_ref):
    _, half, length = blocks_ref.shape
    units = length // 2
    rows = units // 4
    source = lax.broadcasted_iota(jnp.int32, (length, 4 * units), 0)
    target = lax.broadcasted_iota(jnp.int32, (length, 4 * units), 1)
    for side in range(2):
        inside = source - side * units
        start = (inside // rows) * units + inside % rows
        valid = (inside >= 0) & (inside < units)
        total = None
        for b in range(4):
            place = (valid & (target == start + b * rows)).astype(jnp.float32).astype(jnp.bfloat16)
            stacked = jnp.concatenate([blocks_ref[4 * x + b] for x in range(4)], axis=0)
            moved = jnp.dot(stacked, place, preferred_element_type=jnp.float32)
            total = moved if total is None else total + moved
        total = total.astype(jnp.bfloat16)
        for x in range(4):
            update_ref[side * half : (side + 1) * half, x * 4 * units : (x + 1) * 4 * units] = total[
                x * half : (x + 1) * half, :
            ]


def per_device(cotangent, activations, live_mask, projector, first_moment, second_moment):
    width, rank = projector.shape
    own = lax.axis_index("dp")
    tokens, hidden = activations.shape
    rows, pieces = hidden // 64, width // WIDTH_STEP
    factor = 1.0 / math.sqrt(tokens * lax.axis_size("dp"))
    vmem, hbm = pl.BlockSpec(memory_space=pltpu.VMEM), pl.BlockSpec(memory_space=pltpu.HBM)
    parts = pl.pallas_call(
        functools.partial(term_kernel, factor),
        out_shape=jax.ShapeDtypeStruct((16, 4 * rows, rank), jnp.bfloat16),
        in_specs=[vmem, hbm, hbm, hbm],
        out_specs=vmem,
        scratch_shapes=[
            pltpu.VMEM((tokens, width), jnp.bfloat16),
            pltpu.VMEM((tokens, hidden), jnp.bfloat16),
            pltpu.VMEM((hidden, tokens), jnp.bfloat16),
            pltpu.VMEM((width, rank), jnp.bfloat16),
            pltpu.VMEM((tokens, rank), jnp.float32),
            pltpu.SemaphoreType.DMA((pieces,)),
            pltpu.SemaphoreType.DMA,
            pltpu.SemaphoreType.DMA((pieces,)),
        ],
        compiler_params=pltpu.CompilerParams(vmem_limit_bytes=60 * 2**20),
        name="term",
    )(live_mask, cotangent, activations, projector)
    parts = lax.all_to_all(parts, "dp", 0, 0, axis_index_groups=NEAR, tiled=True)
    partial = jnp.sum(parts.astype(jnp.float32), axis=0)

    def swap(pairs, sums, first, second):
        note = jnp.concatenate([sums, first, second], axis=0).astype(jnp.bfloat16)
        return lax.ppermute(note, "dp", pairs)

    other = swap(SWAP_EIGHT, partial, first_moment, second_moment).astype(jnp.float32)
    sums = partial + other[: 4 * rows]
    own_far = (own // 4) % 4
    low = own_far < 2

    def pair(mine, yours):
        return jnp.concatenate([jnp.where(low, mine, yours), jnp.where(low, yours, mine)], axis=0)

    first = pair(first_moment, other[4 * rows : 5 * rows])
    second = pair(second_moment, other[5 * rows :])
    other = swap(SWAP_FOUR, sums, first, second)
    band = width // 64
    bands = lax.dynamic_index_in_dim(projector.reshape(4, 4, 4, band, rank), own_far, 1, False)
    new_first, new_second, blocks = pl.pallas_call(
        step_kernel,
        out_shape=[
            jax.ShapeDtypeStruct((rows, rank), jnp.float32),
            jax.ShapeDtypeStruct((rows, rank), jnp.float32),
            jax.ShapeDtypeStruct((16, band // 2, 8 * rows), jnp.bfloat16),
        ],
        in_specs=[vmem] * 5,
        out_specs=[vmem] * 3,
        compiler_params=pltpu.CompilerParams(vmem_limit_bytes=8 * 2**20),
        name="step",
    )(sums, first, second, other, bands.reshape(16, band, rank))
    blocks = lax.all_to_all(blocks, "dp", 0, 0, axis_index_groups=NEAR, tiled=True)
    update = pl.pallas_call(
        order_kernel,
        out_shape=jax.ShapeDtypeStruct((band, 64 * rows), jnp.bfloat16),
        in_specs=[vmem],
        out_specs=vmem,
        compiler_params=pltpu.CompilerParams(vmem_limit_bytes=4 * 2**20),
        name="order",
    )(blocks)
    return (new_first, new_second, update)


def solution(mesh):
    in_specs = (
        P("dp", None),
        P("dp", "mp"),
        P("dp"),
        P(),
        P(("mp", "dp"), None),
        P(("mp", "dp"), None),
    )
    out_specs = (P(("mp", "dp"), None), P(("mp", "dp"), None), P("dp", "mp"))
    return jax.shard_map(
        per_device, mesh=mesh, in_specs=in_specs, out_specs=out_specs, check_vma=False
    )
```

```python
import functools
import math

import jax
import jax.numpy as jnp
from jax import lax
from jax.experimental import pallas as pl
from jax.experimental.pallas import tpu as pltpu
from jax.sharding import PartitionSpec as P

beta_one = 0.9
beta_two = 0.95
corr_one = 0.99997343860111
corr_two = 0.99407947077967
adam_eps = 1e-08

NEAR = [[16 * x + 4 * a + b for x in range(4) for b in range(4)] for a in range(4)]
FAR = [[16 * x + 4 * a + b for a in range(4)] for x in range(4) for b in range(4)]
SWAP_EIGHT = [(d, d ^ 8) for d in range(64)]
SWAP_FOUR = [(d, d ^ 4) for d in range(64)]


WIDTH_STEP = 1024


def adam(first, second, gradient):
    new_first = beta_one * first + (1.0 - beta_one) * gradient
    new_second = beta_two * second + (1.0 - beta_two) * gradient * gradient
    direction = new_first / corr_one / (jnp.sqrt(new_second / corr_two) + adam_eps)
    return new_first, new_second, direction.astype(jnp.bfloat16)


def term_kernel(factor, mask_ref, cot_hbm, act_hbm, proj_hbm, parts_ref, cot, act, turned, proj, total, cot_sem, act_sem, proj_sem):
    tokens, width = cot.shape
    hidden, rank = act.shape[1], proj.shape[1]
    pieces = width // WIDTH_STEP

    def cot_copy(k):
        at = (slice(None), pl.ds(k * WIDTH_STEP, WIDTH_STEP))
        return pltpu.make_async_copy(cot_hbm.at[at], cot.at[at], cot_sem.at[k])

    def proj_copy(k):
        at = pl.ds(k * WIDTH_STEP, WIDTH_STEP)
        return pltpu.make_async_copy(proj_hbm.at[at], proj.at[at], proj_sem.at[k])

    act_copy = pltpu.make_async_copy(act_hbm, act, act_sem)
    ahead = 3

    def start(k):
        if k < pieces:
            proj_copy(k).start()
            cot_copy(k).start()
        if k == 2:
            act_copy.start()

    for k in range(ahead):
        start(k)
    ones = jnp.ones((8, rank), jnp.bfloat16)
    mask = jnp.broadcast_to(mask_ref[...].astype(jnp.float32)[None, :], (8, tokens))
    mask8 = jnp.where(lax.broadcasted_iota(jnp.int32, mask.shape, 0) == 0, mask, 0.0)
    live = lax.dot_general(
        mask8.astype(jnp.bfloat16), ones, (((0,), (0,)), ((), ())), preferred_element_type=jnp.float32
    )
    for k in range(pieces):
        proj_copy(k).wait()
        cot_copy(k).wait()
        start(k + ahead)
        columns = slice(k * WIDTH_STEP, (k + 1) * WIDTH_STEP)
        piece = jnp.dot(cot[:, columns], proj[columns, :], preferred_element_type=jnp.float32)
        if k > 0:
            piece = total[...] + piece
        if k < pieces - 1:
            total[...] = piece
        if k == 2:
            act_copy.wait()
        if k >= 2:
            each = hidden // (pieces - 2)
            units = slice((k - 2) * each, (k - 2 + 1) * each)
            turned[units, :] = act[:, units].T
    weighted = (piece * live).astype(jnp.bfloat16)
    for x in range(4):
        units = slice(x * hidden // 4, (x + 1) * hidden // 4)
        piece = jnp.dot(turned[units, :], weighted, preferred_element_type=jnp.float32)
        done = (piece * factor).astype(jnp.bfloat16).reshape(4, 4, hidden // 64, rank)
        for b in range(4):
            parts_ref[4 * x + b] = done[:, b].reshape(hidden // 16, rank)


def step_kernel(sums_ref, first_ref, second_ref, other_ref, bands_ref, new_first_ref, new_second_ref, blocks_ref):
    own_far = (lax.axis_index("dp") // 4) % 4
    mine = own_far % 2
    units, rank = sums_ref.shape
    rows = units // 4
    directions = []
    for a in range(4):
        here = mine == a % 2
        at = slice((a // 2) * rows, (a // 2 + 1) * rows)
        gradient = sums_ref[a * rows : (a + 1) * rows, :] + other_ref[a * rows : (a + 1) * rows, :].astype(jnp.float32)
        start = units + (a // 2) * rows
        yours = other_ref[start : start + rows, :].astype(jnp.float32)
        first = jnp.where(here, first_ref[at, :], yours)
        yours = other_ref[start + 2 * rows : start + 3 * rows, :].astype(jnp.float32)
        second = jnp.where(here, second_ref[at, :], yours)
        new_first, new_second, direction = adam(first, second, gradient)
        directions.append(direction)
        if a == 0:
            own_first, own_second = new_first, new_second
        else:
            own_first = jnp.where(own_far == a, new_first, own_first)
            own_second = jnp.where(own_far == a, new_second, own_second)
    new_first_ref[...] = own_first
    new_second_ref[...] = own_second
    direction = jnp.concatenate(directions, axis=0)
    none = jnp.zeros_like(direction)
    low, high = jnp.concatenate([direction, none], axis=0), jnp.concatenate([none, direction], axis=0)
    peers, band, _ = bands_ref.shape
    half = band // 2
    down = (((1,), (1,)), ((), ()))
    top = bands_ref[:, :half, :].reshape(peers * half, rank)
    bottom = bands_ref[:, half:, :].reshape(peers * half, rank)
    both = lax.dot_general(top, low, down, preferred_element_type=jnp.float32)
    both += lax.dot_general(bottom, high, down, preferred_element_type=jnp.float32)
    blocks_ref[...] = both.astype(jnp.bfloat16).reshape(peers, half, 2 * units)


def order_kernel(blocks_ref, update_ref):
    _, half, length = blocks_ref.shape
    units = length // 2
    rows = units // 4
    source = lax.broadcasted_iota(jnp.int32, (length, 4 * units), 0)
    target = lax.broadcasted_iota(jnp.int32, (length, 4 * units), 1)
    for side in range(2):
        inside = source - side * units
        start = (inside // rows) * units + inside % rows
        valid = (inside >= 0) & (inside < units)
        total = None
        for b in range(4):
            place = (valid & (target == start + b * rows)).astype(jnp.float32).astype(jnp.bfloat16)
            stacked = jnp.concatenate([blocks_ref[4 * x + b] for x in range(4)], axis=0)
            moved = jnp.dot(stacked, place, preferred_element_type=jnp.float32)
            total = moved if total is None else total + moved
        total = total.astype(jnp.bfloat16)
        for x in range(4):
            update_ref[side * half : (side + 1) * half, x * 4 * units : (x + 1) * 4 * units] = total[
                x * half : (x + 1) * half, :
            ]


def per_device(cotangent, activations, live_mask, projector, first_moment, second_moment):
    width, rank = projector.shape
    own = lax.axis_index("dp")
    tokens, hidden = activations.shape
    rows, pieces = hidden // 64, width // WIDTH_STEP
    factor = 1.0 / math.sqrt(tokens * lax.axis_size("dp"))
    vmem, hbm = pl.BlockSpec(memory_space=pltpu.VMEM), pl.BlockSpec(memory_space=pltpu.HBM)
    parts = pl.pallas_call(
        functools.partial(term_kernel, factor),
        out_shape=jax.ShapeDtypeStruct((16, 4 * rows, rank), jnp.bfloat16),
        in_specs=[vmem, hbm, hbm, hbm],
        out_specs=vmem,
        scratch_shapes=[
            pltpu.VMEM((tokens, width), jnp.bfloat16),
            pltpu.VMEM((tokens, hidden), jnp.bfloat16),
            pltpu.VMEM((hidden, tokens), jnp.bfloat16),
            pltpu.VMEM((width, rank), jnp.bfloat16),
            pltpu.VMEM((tokens, rank), jnp.float32),
            pltpu.SemaphoreType.DMA((pieces,)),
            pltpu.SemaphoreType.DMA,
            pltpu.SemaphoreType.DMA((pieces,)),
        ],
        compiler_params=pltpu.CompilerParams(vmem_limit_bytes=60 * 2**20),
        name="term",
    )(live_mask, cotangent, activations, projector)
    parts = lax.all_to_all(parts, "dp", 0, 0, axis_index_groups=NEAR, tiled=True)
    partial = jnp.sum(parts.astype(jnp.float32), axis=0)

    def swap(pairs, sums, first, second):
        note = jnp.concatenate([sums, first, second], axis=0).astype(jnp.bfloat16)
        return lax.ppermute(note, "dp", pairs)

    other = swap(SWAP_EIGHT, partial, first_moment, second_moment).astype(jnp.float32)
    sums = partial + other[: 4 * rows]
    own_far = (own // 4) % 4
    low = own_far < 2

    def pair(mine, yours):
        return jnp.concatenate([jnp.where(low, mine, yours), jnp.where(low, yours, mine)], axis=0)

    first = pair(first_moment, other[4 * rows : 5 * rows])
    second = pair(second_moment, other[5 * rows :])
    other = swap(SWAP_FOUR, sums, first, second)
    band = width // 64
    bands = lax.dynamic_index_in_dim(projector.reshape(4, 4, 4, band, rank), own_far, 1, False)
    new_first, new_second, blocks = pl.pallas_call(
        step_kernel,
        out_shape=[
            jax.ShapeDtypeStruct((rows, rank), jnp.float32),
            jax.ShapeDtypeStruct((rows, rank), jnp.float32),
            jax.ShapeDtypeStruct((16, band // 2, 8 * rows), jnp.bfloat16),
        ],
        in_specs=[vmem] * 5,
        out_specs=[vmem] * 3,
        compiler_params=pltpu.CompilerParams(vmem_limit_bytes=8 * 2**20),
        name="step",
    )(sums, first, second, other, bands.reshape(16, band, rank))
    blocks = lax.all_to_all(blocks, "dp", 0, 0, axis_index_groups=NEAR, tiled=True)
    update = pl.pallas_call(
        order_kernel,
        out_shape=jax.ShapeDtypeStruct((band, 64 * rows), jnp.bfloat16),
        in_specs=[vmem],
        out_specs=vmem,
        compiler_params=pltpu.CompilerParams(vmem_limit_bytes=4 * 2**20),
        name="order",
    )(blocks)
    return (new_first, new_second, update)


def solution(mesh):
    in_specs = (
        P("dp", None),
        P("dp", "mp"),
        P("dp"),
        P(),
        P(("mp", "dp"), None),
        P(("mp", "dp"), None),
    )
    out_specs = (P(("mp", "dp"), None), P(("mp", "dp"), None), P("dp", "mp"))
    return jax.shard_map(
        per_device, mesh=mesh, in_specs=in_specs, out_specs=out_specs, check_vma=False
    )
```
